32 devices in a mesh: stream: 8 (over z, x), tensor: 4 (over y, core).
Axes of the slice: x: 2, y: 2, z: 4, core: 2. Of those that a mesh axis runs over, the one named last changes fastest.
Arguments:
- hidden: bfloat16 [512, 8192], P('stream', 'tensor'), may hold values from -600 to 600
- norm_gain: bfloat16 [8192], replicated, may hold values from 0.099609375 to 1.8984375
- head_weight: bfloat16 [8192, 128256], P(None, ('stream', 'tensor')), may hold values from -32 to 32
- floor_counts: int32 [128256], P(('stream', 'tensor')), may hold values from 1 to 7
- totals: int32 [512], replicated, may hold values from 1048576 to 4194304
- targets: int32 [512], replicated, may hold values from 0 to 128255
Outputs:
- cumulative: float32 [512, 128256], P(None, ('stream', 'tensor'))
- code_bits: float32 [512], replicated
The draws below stay inside these ranges and needn't reach their ends.
All inputs are finite; a program needn't handle non-finite values.
Results may differ from the reference program's by a relative error of at most 0.0003.
The reference program's roundings to bfloat16 on the way (of `normed`) count: a program that leaves them out, or rounds other values in their place, can miss the bound.
Values may be sent and summed in bfloat16 or wider, within the bound.
A program may use at most 192 MiB of HBM per device.

```python
import jax
import jax.numpy as jnp
from jax import lax

D = 8192
V = 128256
TOK_DEV = 64
TOKENS = 512


def common_anchors(key):
    return jnp.clip(jax.random.normal(jax.random.fold_in(key, 77), (8, D), jnp.float32), -6.0, 6.0)


def anchor_rows(values, base, row_scale, anchors):
    row_index = jnp.arange(TOKENS, dtype=jnp.int32)
    aligned = row_index % 16 == 3
    chosen = anchors[row_index // 16 % 8]
    strength = (0.6 + 0.2 * (row_index // 16 % 3).astype(jnp.float32))[:, None]
    anchored = row_scale * (strength * chosen + (1.0 - strength) * base)
    return jnp.where(aligned[:, None], anchored, values)


def anchor_columns(values, anchors, noise_key, scale):
    block_width = V // 8
    anchor_index = jnp.repeat(jnp.arange(8, dtype=jnp.int32), 2)
    second_col = jnp.arange(16, dtype=jnp.int32) % 2
    column_index = anchor_index * block_width + 5 + second_col * (block_width // 2)
    noise = jnp.clip(jax.random.normal(noise_key, (D, 16), jnp.float32), -6.0, 6.0) * scale
    factor = 1.0 - 0.01 * second_col.astype(jnp.float32)
    columns_new = 250.0 / D * anchors[anchor_index].T * factor[None, :] + noise
    return values.at[:, column_index].set(columns_new)


def draw_hidden(key, part):
    anchors = common_anchors(key)
    key = jax.random.fold_in(key, 1)
    first_key, second_key, third_key = jax.random.split(key, 3)
    row_scale = jnp.exp(jax.random.uniform(first_key, (TOKENS, 1), jnp.float32) * jnp.log(10.0))
    column_scale = jnp.exp(jax.random.uniform(second_key, (1, D), jnp.float32) * jnp.log(10.0))
    base = jnp.clip(jax.random.normal(third_key, (TOKENS, D), jnp.float32), -6.0, 6.0)
    values = base * row_scale * column_scale
    values = anchor_rows(values, base, row_scale, anchors)
    return values.astype(jnp.bfloat16)


def draw_head_weight(key, part):
    anchors = common_anchors(key)
    key = jax.random.fold_in(key, 2)
    first_key, second_key = jax.random.split(key, 2)
    scale = 3.0 / D ** 0.5
    values = jnp.clip(jax.random.normal(first_key, (D, V), jnp.float32), -6.0, 6.0) * scale
    values = anchor_columns(values, anchors, second_key, scale)
    return values.astype(jnp.bfloat16)


def draw_floor_counts(key, part):
    key = jax.random.fold_in(key, 3)
    entries = jnp.arange(V, dtype=jnp.int32)
    upper = 1 + 6 * entries // V
    extra = jax.random.randint(key, (V,), 0, upper)
    counts = 1 + extra
    return jnp.where(entries == V - 1, 7, counts).astype(jnp.int32)


def touch_ends(result, stream_key, low, high):
    shape = result.shape
    place = [jax.random.randint(jax.random.fold_in(stream_key, axis), (), 0, shape[axis]) for axis in range(len(shape))]
    result = result.at[tuple(place)].set(low)
    longest = shape.index(max(shape))
    place[longest] = (place[longest] + 1) % shape[longest]
    return result.at[tuple(place)].set(high)


def setup_inputs(seed: int = 0) -> dict:
    arg_keys = jax.random.split(jax.random.key(seed), 7)
    hidden = draw_hidden(jax.random.fold_in(arg_keys[6], 71), 0)
    norm_gain = jnp.clip(1.0 + 0.18 * jax.random.normal(arg_keys[1], (D,), jnp.float32), 0.099609375, 1.8984375).astype(jnp.bfloat16)
    head_weight = draw_head_weight(jax.random.fold_in(arg_keys[6], 71), 0)
    floor_counts = draw_floor_counts(jax.random.fold_in(arg_keys[6], 71), 0)
    totals = touch_ends(jax.random.randint(arg_keys[4], (TOKENS,), 1048576, 4194305), jax.random.fold_in(arg_keys[4], 1), 1048576, 4194304).astype(jnp.int32)
    targets = touch_ends(jax.random.randint(arg_keys[5], (TOKENS,), 0, V), jax.random.fold_in(arg_keys[5], 1), 0, V - 1).astype(jnp.int32)
    return {"hidden": hidden, "norm_gain": norm_gain, "head_weight": head_weight, "floor_counts": floor_counts, "totals": totals, "targets": targets}


epsilon = 1e-05

def reference(hidden, norm_gain, head_weight, floor_counts, totals, targets):
    widened = hidden.astype(jnp.float32)
    mean_square = lax.optimization_barrier(jnp.mean(widened * widened, axis=1, keepdims=True))
    normed = (widened * lax.rsqrt(mean_square + epsilon) * norm_gain.astype(jnp.float32)[None, :]).astype(jnp.bfloat16)
    floor_float = floor_counts.astype(jnp.float32)
    floor_sum = jnp.sum(floor_float)
    columns = jnp.arange(V, dtype=jnp.int32)

    def per_block(operands):
        block_rows, block_totals, block_targets = operands
        logits = jnp.dot(block_rows, head_weight, preferred_element_type=jnp.float32)
        row_peak = lax.optimization_barrier(jnp.max(logits, axis=1, keepdims=True))
        exponent = jnp.exp(logits - row_peak)
        probabilities = exponent / lax.optimization_barrier(jnp.sum(exponent, axis=1, keepdims=True))
        token_total = block_totals.astype(jnp.float32)[:, None]
        quantized = (floor_float[None, :] + probabilities * (token_total - floor_sum)) / token_total
        running = jnp.cumsum(quantized, axis=1)
        cumulative = jnp.concatenate([jnp.zeros((quantized.shape[0], 1), quantized.dtype), running[:, :-1]], axis=1)
        picked = lax.optimization_barrier(jnp.sum(jnp.where(columns[None, :] == block_targets[:, None], quantized, 0.0), axis=1))
        return (cumulative, -jnp.log2(picked))
    blocks = TOKENS // TOK_DEV
    cumulative, code_bits = lax.map(per_block, (normed.reshape(blocks, TOK_DEV, D), totals.reshape(blocks, TOK_DEV), targets.reshape(blocks, TOK_DEV)))
    return (cumulative.reshape(TOKENS, V), code_bits.reshape(TOKENS))
```

```python
import functools

import jax
import jax.numpy as jnp
from jax import lax
from jax.experimental import pallas as pl
from jax.experimental.pallas import tpu as pltpu
from jax.sharding import PartitionSpec as P

epsilon = 1e-05
BLOCK = 256
BOTH = ("stream", "tensor")


def blocks_of(width):
    return [(start, min(BLOCK, width - start)) for start in range(0, width, BLOCK)]


def strict_upper(size):
    row = lax.broadcasted_iota(jnp.int32, (size, size), 0)
    col = lax.broadcasted_iota(jnp.int32, (size, size), 1)
    return jnp.where(row < col, 1.0, 0.0).astype(jnp.bfloat16)


def running_sum(value, upper, emit):
    rows, width = value.shape
    total = jnp.zeros((rows, 1), jnp.float32)
    for start, size in blocks_of(width):
        piece = value[:, start : start + size]
        high = piece.astype(jnp.bfloat16)
        low = (piece - high.astype(jnp.float32)).astype(jnp.bfloat16)
        within = jnp.dot(
            jnp.concatenate([high, low], axis=0), upper[:size, :size], preferred_element_type=jnp.float32
        )
        emit(start, size, total + (within[:rows] + within[rows:]))
        total += jnp.sum(piece, axis=1, keepdims=True)
    return total


def post_kernel(logits_ref, floor_ref, target_ref, running_ref, floor_running_ref, stats_ref):
    logits = logits_ref[...]
    rows, width = logits.shape
    peak = jnp.max(logits, axis=1, keepdims=True)
    exponent = jnp.exp(logits - peak)
    hit = lax.broadcasted_iota(jnp.int32, (rows, width), 1) == target_ref[...]
    picked = jnp.sum(jnp.where(hit, exponent, 0.0), axis=1, keepdims=True)
    floor = floor_ref[...]
    floor_picked = jnp.sum(jnp.where(hit, floor[:1], 0.0), axis=1, keepdims=True)

    def emit(start, size, piece):
        running_ref[:, start : start + size] = piece

    mass = running_sum(exponent, strict_upper(BLOCK), emit)

    def emit_floor(start, size, piece):
        floor_running_ref[:, start : start + size] = piece

    floor_mass = running_sum(floor, strict_upper(BLOCK), emit_floor)
    lane = lax.broadcasted_iota(jnp.int32, stats_ref.shape, 1)
    stats = jnp.where(lane == 0, peak, 0.0)
    stats = jnp.where(lane == 1, mass, stats)
    stats = jnp.where(lane == 2, picked, stats)
    stats = jnp.where(lane == 3, floor_picked, stats)
    stats = jnp.where(lane == 4, floor_mass[:1], stats)
    stats_ref[...] = stats


def post(logits, floor, target):
    tokens, width = logits.shape
    rows = 64
    return pl.pallas_call(
        post_kernel,
        grid=(tokens // rows,),
        in_specs=[
            pl.BlockSpec((rows, width), lambda i: (i, 0)),
            pl.BlockSpec((8, width), lambda i: (0, 0)),
            pl.BlockSpec((rows, 1), lambda i: (i, 0)),
        ],
        out_specs=[
            pl.BlockSpec((rows, width), lambda i: (i, 0)),
            pl.BlockSpec((8, width), lambda i: (0, 0)),
            pl.BlockSpec((rows, 128), lambda i: (i, 0)),
        ],
        out_shape=[
            jax.ShapeDtypeStruct((tokens, width), jnp.float32),
            jax.ShapeDtypeStruct((8, width), jnp.float32),
            jax.ShapeDtypeStruct((tokens, 128), jnp.float32),
        ],
        compiler_params=pltpu.CompilerParams(vmem_limit_bytes=40 * 2**20),
        cost_estimate=pl.CostEstimate(
            flops=4 * tokens * width * BLOCK, bytes_accessed=8 * tokens * width, transcendentals=tokens * width
        ),
    )(logits, floor, target)


def finish(stats, running, floor_running, totals, mine):
    peak, mass, picked, floor_picked, floor_mass = (stats[:, i] for i in range(5))
    total = totals.astype(jnp.float32)
    row_peak = jnp.max(peak, axis=0)
    lift = jnp.exp(peak - row_peak[None])
    row_mass = jnp.sum(mass * lift, axis=0)
    floor_sum = jnp.sum(floor_mass[:, :1])
    share = (total - floor_sum) / (row_mass * total)
    scale = lift * share[None]
    block_sum = floor_mass / total[None] + mass * scale
    below = (jnp.arange(peak.shape[0]) < mine)[:, None]
    offset = jnp.sum(jnp.where(below, block_sum, 0.0), axis=0)
    target_mass = jnp.sum(floor_picked / total[None] + picked * scale, axis=0)
    my_scale = jnp.sum(jnp.where((jnp.arange(peak.shape[0]) == mine)[:, None], scale, 0.0), axis=0)
    cumulative = offset[:, None] + floor_running[:1] * (1.0 / total)[:, None] + running * my_scale[:, None]
    return cumulative, -jnp.log2(target_mass)


def local(hidden, norm_gain, head_weight, floor_counts, totals, targets):
    vocab_width = head_weight.shape[1]
    mine = lax.axis_index(BOTH)
    depth = hidden.shape[1]
    widened = hidden.astype(jnp.float32)
    square = lax.psum(jnp.sum(widened * widened, axis=1, keepdims=True), "tensor")
    mean_square = square / (depth * lax.axis_size("tensor"))
    gain = lax.dynamic_slice(norm_gain, (lax.axis_index("tensor") * depth,), (depth,))
    normed = (widened * lax.rsqrt(mean_square + epsilon) * gain.astype(jnp.float32)[None, :]).astype(jnp.bfloat16)
    normed = lax.all_gather(normed, "tensor", axis=1, tiled=True)
    normed = lax.all_gather(normed, "stream", axis=0, tiled=True)
    logits = jnp.dot(normed, head_weight, preferred_element_type=jnp.float32)
    floor = jnp.broadcast_to(floor_counts.astype(jnp.float32)[None, :], (8, vocab_width))
    target = (targets - mine * vocab_width)[:, None]
    running, floor_running, stats = post(logits, floor, target)
    stats = lax.all_gather(stats[:, :8].T, BOTH)
    return finish(stats, running, floor_running, totals, mine)


MESH = pl.DeviceIdType.MESH
PARTS = 4
SLOTS = 8
TILE = 1024


def head_kernel(
    devices, hidden_ref, gain_ref, weight_ref, floor_ref, target_ref, total_ref,
    running_ref, floor_running_ref, scales_ref, bits_ref,
    acts, acc, weights, upper, squares, stats, columns,
    square_send, square_recv, line_send, line_recv, first_send, first_recv,
    second_send, second_recv, pair_send, pair_recv, stats_send, stats_recv, weight_sem, out_sem,
):
    rows, depth = hidden_ref.shape
    tokens, width = acc.shape
    part = depth // PARTS
    deep = acts.shape[0] // PARTS
    line = tokens // rows // 2
    stream, tensor = lax.axis_index("stream"), lax.axis_index("tensor")
    place, side = stream // 2, stream % 2
    level, core = tensor // 2, tensor % 2
    me = stream * deep + tensor
    first_side, first_level = (side + core) % 2, (level + 1 - core) % 2
    second_side, second_level = (side + 1 - core) % 2, (level + core) % 2
    far_level = (level + 1) % 2
    first_to = (place * 2 + first_side, first_level * 2 + core)
    second_to = (place * 2 + second_side, second_level * 2 + core)
    pair_to = (stream, level * 2 + 1 - core)

    barrier = pltpu.get_barrier_semaphore()

    def greet(step, carry):
        other = (me + step) % devices
        pl.semaphore_signal(barrier, inc=1, device_id=(other // deep, other % deep), device_id_type=MESH)
        return carry

    lax.fori_loop(1, devices, greet, 0)

    def chunk_of(step):
        turn, kind = step // 4, step % 4
        at_level = (level + kind % 2) % 2
        at_core = (core + kind // 2) % 2
        return (at_level * 2 + at_core) * PARTS + turn

    def weight_copy(step):
        start = pl.multiple_of(chunk_of(step) * part, part)
        slot = step % SLOTS
        return pltpu.make_async_copy(weight_ref.at[pl.ds(start, part), :], weights.at[slot], weight_sem.at[slot])

    steps = deep * PARTS

    def first_weights(step, carry):
        weight_copy(step).start()
        return carry

    lax.fori_loop(0, SLOTS, first_weights, 0)

    def block(at_place, at_side, at_tensor, turn):
        start = pl.multiple_of((at_place * 2 + at_side) * rows, rows)
        return acts.at[at_tensor * PARTS + turn, pl.ds(start, rows), :]

    def send(ref, send_sem, recv_sem, to):
        return pltpu.make_async_remote_copy(
            src_ref=ref, dst_ref=ref, send_sem=send_sem, recv_sem=recv_sem, device_id=to, device_id_type=MESH
        )

    def line_copy(at_place, turn, to_place):
        return send(
            block(at_place, side, tensor, turn),
            line_send.at[turn, to_place], line_recv.at[turn, at_place], (to_place * 2 + side, tensor),
        )

    def first_copy(at_place, at_side, at_level, turn):
        return send(
            block(at_place, at_side, at_level * 2 + core, turn),
            first_send.at[turn, at_place], first_recv.at[turn, at_place], first_to,
        )

    def second_copy(at_place, at_side, at_level, turn, index):
        return send(
            block(at_place, at_side, at_level * 2 + core, turn),
            second_send.at[turn, index], second_recv.at[turn, index], second_to,
        )

    def pair_copy(at_tensor, turn, index):
        return send(
            acts.at[at_tensor * PARTS + turn], pair_send.at[turn, index], pair_recv.at[turn, index], pair_to
        )

    hidden = hidden_ref[...].astype(jnp.float32)
    squares[tensor] = jnp.broadcast_to(jnp.sum(hidden * hidden, axis=1, keepdims=True), squares.shape[1:])
    pl.semaphore_wait(barrier, devices - 1)

    def square_copy(of, to):
        return send(squares.at[of], square_send.at[to], square_recv.at[of], (stream, to))

    for step in range(1, deep):
        square_copy(tensor, (tensor + step) % deep).start()

    row = lax.broadcasted_iota(jnp.int32, upper.shape, 0)
    col = lax.broadcasted_iota(jnp.int32, upper.shape, 1)
    upper[...] = jnp.where(row < col, 1.0, 0.0).astype(jnp.bfloat16)
    acc[...] = jnp.zeros_like(acc)
    for step in range(1, deep):
        square_copy((tensor + step) % deep, tensor).wait_recv()
    square = jnp.sum(squares[...], axis=0)[:, :1]
    factor = lax.rsqrt(square / (depth * deep) + epsilon)
    for turn in range(PARTS):
        at = slice(turn * part, (turn + 1) * part)
        gain = gain_ref[pl.ds(tensor, 1), at].astype(jnp.float32)
        normed = hidden_ref[:, at].astype(jnp.float32) * factor * gain
        start = pl.multiple_of(stream * rows, rows)
        acts[tensor * PARTS + turn, pl.ds(start, rows), :] = normed.astype(jnp.bfloat16)
        for step in range(1, line):
            line_copy(place, turn, (place + step) % line).start()
        first_copy(place, side, level, turn).start()
        second_copy(place, side, level, turn, place).start()

    def pass_line(turn):
        def go(step, carry):
            at = (place + step) % line
            line_copy(at, turn, place).wait_recv()
            first_copy(at, side, level, turn).start()
            second_copy(at, side, level, turn, at).start()
            return carry

        lax.fori_loop(1, line, go, 0)

    def pass_first(turn):
        def go(step, carry):
            at = (place + step) % line
            first_copy(at, first_side, first_level, turn).wait_recv()
            second_copy(at, first_side, first_level, turn, line + at).start()
            return carry

        lax.fori_loop(0, line, go, 0)

    def pass_second(turn):
        def go(step, carry):
            at = (place + step) % line
            second_copy(at, second_side, second_level, turn, at).wait_recv()
            return carry

        def go_far(step, carry):
            at = (place + step) % line
            second_copy(at, (side + 1) % 2, far_level, turn, line + at).wait_recv()
            return carry

        lax.fori_loop(0, line, go, 0)
        lax.fori_loop(0, line, go_far, 0)
        pair_copy(tensor, turn, 0).start()
        pair_copy(far_level * 2 + core, turn, 1).start()

    pass_line(0)
    pass_first(0)
    pass_line(1)
    pass_second(0)

    def multiply(step, carry):
        turn, kind = step // 4, step % 4

        @pl.when((kind == 0) & (turn + 2 < PARTS))
        def _():
            pass_line(turn + 2)

        @pl.when((kind == 0) & (turn + 1 < PARTS))
        def _():
            pass_first(turn + 1)

        @pl.when(kind == 2)
        def _():
            pair_copy(level * 2 + 1 - core, turn, 0).wait_recv()
            pair_copy(far_level * 2 + 1 - core, turn, 1).wait_recv()

        weight_copy(step).wait()
        chunk, slot = chunk_of(step), step % SLOTS
        for start in range(0, width, TILE):
            at = slice(start, min(start + TILE, width))
            acc[:, at] += jnp.dot(acts[chunk], weights[slot, :, at], preferred_element_type=jnp.float32)

        @pl.when(step + SLOTS < steps)
        def _():
            weight_copy(step + SLOTS).start()

        @pl.when((kind == 3) & (turn + 1 < PARTS))
        def _():
            pass_second(turn + 1)

        return carry

    lax.fori_loop(0, steps, multiply, 0)

    floor = floor_ref[...]
    floor_mass = jnp.sum(floor[:1], axis=1, keepdims=True)
    small = 32

    def measure(step, carry):
        at = pl.ds(pl.multiple_of(step * small, small), small)
        logits = acc[at, :]
        peak = jnp.max(logits, axis=1, keepdims=True)
        exponent = jnp.exp(logits - peak)
        acc[at, :] = exponent
        hit = lax.broadcasted_iota(jnp.int32, (small, width), 1) == target_ref[at, :]
        picked = jnp.sum(jnp.where(hit, exponent, 0.0), axis=1, keepdims=True)
        floor_picked = jnp.sum(jnp.where(hit, floor_ref[:1, :], 0.0), axis=1, keepdims=True)
        mass = jnp.sum(exponent, axis=1, keepdims=True)
        lane = lax.broadcasted_iota(jnp.int32, (small, 128), 1)
        value = jnp.where(lane == 0, peak, 0.0)
        value = jnp.where(lane == 1, mass, value)
        value = jnp.where(lane == 2, picked, value)
        value = jnp.where(lane == 3, floor_picked, value)
        columns[at, :] = jnp.where(lane == 4, floor_mass, value)
        return carry

    lax.fori_loop(0, tokens // small, measure, 0)
    stats[me] = columns[...].T[:8]

    def stats_copy(of, to):
        return send(stats.at[of], stats_send.at[to], stats_recv.at[of], (to // deep, to % deep))

    def share(step, carry):
        stats_copy(me, (me + step) % devices).start()
        return carry

    lax.fori_loop(1, devices, share, 0)

    def emit_floor(start, size, piece):
        floor_running_ref[:, start : start + size] = piece

    running_sum(floor, upper, emit_floor)
    large = 128

    def out_copy(step):
        at = pl.ds(pl.multiple_of(step * large, large), large)
        return pltpu.make_async_copy(acc.at[at, :], running_ref.at[at, :], out_sem.at[step])

    def accumulate(step, carry):
        at = pl.ds(pl.multiple_of(step * large, large), large)

        def emit(start, size, piece):
            acc[at, start : start + size] = piece

        running_sum(acc.at[at, :], upper, emit)
        out_copy(step).start()
        return carry

    lax.fori_loop(0, tokens // large, accumulate, 0)

    def settle(step, carry):
        stats_copy((me + step) % devices, me).wait_recv()
        return carry

    lax.fori_loop(1, devices, settle, 0)
    peak, mass, picked, floor_picked, floor_all = (stats[:, i, :] for i in range(5))
    total = total_ref[...].astype(jnp.float32)
    lift = jnp.exp(peak - jnp.max(peak, axis=0, keepdims=True))
    row_mass = jnp.sum(mass * lift, axis=0, keepdims=True)
    floor_sum = jnp.sum(floor_all, axis=0, keepdims=True)
    scale = lift * ((total - floor_sum) / (row_mass * total))
    device = lax.broadcasted_iota(jnp.int32, peak.shape, 0)
    block_sum = floor_all / total + mass * scale
    offset = jnp.sum(jnp.where(device < me, block_sum, 0.0), axis=0, keepdims=True)
    my_scale = jnp.sum(jnp.where(device == me, scale, 0.0), axis=0, keepdims=True)
    target_mass = jnp.sum(floor_picked / total + picked * scale, axis=0, keepdims=True)
    bits_ref[...] = -(jnp.log(target_mass) / 0.6931471805599453)
    lane = lax.broadcasted_iota(jnp.int32, (128, tokens), 0)
    value = jnp.where(lane == 0, offset, 0.0)
    value = jnp.where(lane == 1, 1.0 / total, value)
    value = jnp.where(lane == 2, my_scale, value)
    scales_ref[...] = value.T

    for step in range(1, deep):
        square_copy(tensor, (tensor + step) % deep).wait_send()

    def sent(turn, carry):
        def go_line(step, carry):
            line_copy(place, turn, (place + step) % line).wait_send()
            return carry

        def go(step, carry):
            first_copy(step, side, level, turn).wait_send()
            second_copy(step, side, level, turn, step).wait_send()
            second_copy(step, first_side, first_level, turn, line + step).wait_send()
            return carry

        lax.fori_loop(1, line, go_line, 0)
        lax.fori_loop(0, line, go, 0)
        pair_copy(tensor, turn, 0).wait_send()
        pair_copy(far_level * 2 + core, turn, 1).wait_send()
        return carry

    lax.fori_loop(0, PARTS, sent, 0)

    def stats_sent(step, carry):
        stats_copy(me, (me + step) % devices).wait_send()
        return carry

    lax.fori_loop(1, devices, stats_sent, 0)

    def out_done(step, carry):
        out_copy(step).wait()
        return carry

    lax.fori_loop(0, tokens // large, out_done, 0)


def head(hidden, gain, weight, floor, target, total):
    rows, depth = hidden.shape
    streams, deep = lax.axis_size("stream"), lax.axis_size("tensor")
    devices, line = streams * deep, streams // 2
    tokens, width = streams * rows, weight.shape[1]
    part = depth // PARTS
    vmem = pl.BlockSpec(memory_space=pltpu.VMEM)
    anywhere = pl.BlockSpec(memory_space=pl.ANY)
    dma = pltpu.SemaphoreType.DMA
    return pl.pallas_call(
        functools.partial(head_kernel, devices),
        in_specs=[vmem, vmem, anywhere, vmem, vmem, vmem],
        out_specs=[anywhere, vmem, vmem, vmem],
        out_shape=[
            jax.ShapeDtypeStruct((tokens, width), jnp.float32),
            jax.ShapeDtypeStruct((8, width), jnp.float32),
            jax.ShapeDtypeStruct((tokens, 128), jnp.float32),
            jax.ShapeDtypeStruct((1, tokens), jnp.float32),
        ],
        scratch_shapes=[
            pltpu.VMEM((deep * PARTS, tokens, part), jnp.bfloat16),
            pltpu.VMEM((tokens, width), jnp.float32),
            pltpu.VMEM((SLOTS, part, width), jnp.bfloat16),
            pltpu.VMEM((BLOCK, BLOCK), jnp.bfloat16),
            pltpu.VMEM((deep, rows, 128), jnp.float32),
            pltpu.VMEM((devices, 8, tokens), jnp.float32),
            pltpu.VMEM((tokens, 128), jnp.float32),
            dma((deep,)), dma((deep,)),
            dma((PARTS, line)), dma((PARTS, line)),
            dma((PARTS, line)), dma((PARTS, line)),
            dma((PARTS, 2 * line)), dma((PARTS, 2 * line)),
            dma((PARTS, 2)), dma((PARTS, 2)),
            dma((devices,)), dma((devices,)),
            dma((SLOTS,)), dma((tokens // 128,)),
        ],
        compiler_params=pltpu.CompilerParams(
            collective_id=0, has_side_effects=True, vmem_limit_bytes=62 * 2**20
        ),
        cost_estimate=pl.CostEstimate(
            flops=2 * tokens * depth * deep * width,
            bytes_accessed=2 * depth * deep * width + 4 * tokens * width,
            transcendentals=tokens * width,
        ),
    )(hidden, gain, weight, floor, target, total)


def finish_kernel(running_ref, floor_running_ref, scales_ref, out_ref):
    scales = scales_ref[...]
    out_ref[...] = scales[:, :1] + floor_running_ref[:1, :] * scales[:, 1:2] + running_ref[...] * scales[:, 2:3]


def finish_local(running, floor_running, scales):
    tokens, width = running.shape
    rows = 64
    tile = pl.BlockSpec((rows, width), lambda i: (i, 0))
    return pl.pallas_call(
        finish_kernel,
        grid=(tokens // rows,),
        in_specs=[tile, pl.BlockSpec((8, width), lambda i: (0, 0)), pl.BlockSpec((rows, 128), lambda i: (i, 0))],
        out_specs=tile,
        out_shape=jax.ShapeDtypeStruct((tokens, width), jnp.float32),
        compiler_params=pltpu.CompilerParams(vmem_limit_bytes=40 * 2**20),
        cost_estimate=pl.CostEstimate(flops=4 * tokens * width, bytes_accessed=8 * tokens * width, transcendentals=0),
    )(running, floor_running, scales)


def local_fused(hidden, norm_gain, head_weight, floor_counts, totals, targets):
    vocab_width = head_weight.shape[1]
    mine = lax.axis_index(BOTH)
    floor = jnp.broadcast_to(floor_counts.astype(jnp.float32)[None, :], (8, vocab_width))
    target = (targets - mine * vocab_width)[:, None]
    gain = norm_gain.astype(jnp.float32).reshape(-1, hidden.shape[1])
    running, floor_running, scales, bits = head(hidden, gain, head_weight, floor, target, totals[None, :])
    return finish_local(running, floor_running, scales), bits[0]


def solution(mesh):
    in_specs = (P("stream", "tensor"), P(), P(None, BOTH), P(BOTH), P(), P())
    out_specs = (P(None, BOTH), P())
    fused = mesh.shape["tensor"] == 4 and mesh.shape["stream"] % 2 == 0 and mesh.shape["stream"] <= 8
    body = local_fused if fused else local
    return jax.shard_map(body, mesh=mesh, in_specs=in_specs, out_specs=out_specs, check_vma=False)
```

```python
import functools

import jax
import jax.numpy as jnp
from jax import lax
from jax.experimental import pallas as pl
from jax.experimental.pallas import tpu as pltpu
from jax.sharding import PartitionSpec as P

epsilon = 1e-05
BLOCK = 256
BOTH = ("stream", "tensor")


def blocks_of(width):
    return [(start, min(BLOCK, width - start)) for start in range(0, width, BLOCK)]


def strict_upper(size):
    row = lax.broadcasted_iota(jnp.int32, (size, size), 0)
    col = lax.broadcasted_iota(jnp.int32, (size, size), 1)
    return jnp.where(row < col, 1.0, 0.0).astype(jnp.bfloat16)


def running_sum(value, upper, emit):
    rows, width = value.shape
    total = jnp.zeros((rows, 1), jnp.float32)
    for start, size in blocks_of(width):
        piece = value[:, start : start + size]
        high = piece.astype(jnp.bfloat16)
        low = (piece - high.astype(jnp.float32)).astype(jnp.bfloat16)
        within = jnp.dot(
            jnp.concatenate([high, low], axis=0), upper[:size, :size], preferred_element_type=jnp.float32
        )
        emit(start, size, total + (within[:rows] + within[rows:]))
        total += jnp.sum(piece, axis=1, keepdims=True)
    return total


def post_kernel(logits_ref, floor_ref, target_ref, running_ref, floor_running_ref, stats_ref):
    logits = logits_ref[...]
    rows, width = logits.shape
    peak = jnp.max(logits, axis=1, keepdims=True)
    exponent = jnp.exp(logits - peak)
    hit = lax.broadcasted_iota(jnp.int32, (rows, width), 1) == target_ref[...]
    picked = jnp.sum(jnp.where(hit, exponent, 0.0), axis=1, keepdims=True)
    floor = floor_ref[...]
    floor_picked = jnp.sum(jnp.where(hit, floor[:1], 0.0), axis=1, keepdims=True)

    def emit(start, size, piece):
        running_ref[:, start : start + size] = piece

    mass = running_sum(exponent, strict_upper(BLOCK), emit)

    def emit_floor(start, size, piece):
        floor_running_ref[:, start : start + size] = piece

    floor_mass = running_sum(floor, strict_upper(BLOCK), emit_floor)
    lane = lax.broadcasted_iota(jnp.int32, stats_ref.shape, 1)
    stats = jnp.where(lane == 0, peak, 0.0)
    stats = jnp.where(lane == 1, mass, stats)
    stats = jnp.where(lane == 2, picked, stats)
    stats = jnp.where(lane == 3, floor_picked, stats)
    stats = jnp.where(lane == 4, floor_mass[:1], stats)
    stats_ref[...] = stats


def post(logits, floor, target):
    tokens, width = logits.shape
    rows = 64
    return pl.pallas_call(
        post_kernel,
        grid=(tokens // rows,),
        in_specs=[
            pl.BlockSpec((rows, width), lambda i: (i, 0)),
            pl.BlockSpec((8, width), lambda i: (0, 0)),
            pl.BlockSpec((rows, 1), lambda i: (i, 0)),
        ],
        out_specs=[
            pl.BlockSpec((rows, width), lambda i: (i, 0)),
            pl.BlockSpec((8, width), lambda i: (0, 0)),
            pl.BlockSpec((rows, 128), lambda i: (i, 0)),
        ],
        out_shape=[
            jax.ShapeDtypeStruct((tokens, width), jnp.float32),
            jax.ShapeDtypeStruct((8, width), jnp.float32),
            jax.ShapeDtypeStruct((tokens, 128), jnp.float32),
        ],
        compiler_params=pltpu.CompilerParams(vmem_limit_bytes=40 * 2**20),
        cost_estimate=pl.CostEstimate(
            flops=4 * tokens * width * BLOCK, bytes_accessed=8 * tokens * width, transcendentals=tokens * width
        ),
    )(logits, floor, target)


def finish(stats, running, floor_running, totals, mine):
    peak, mass, picked, floor_picked, floor_mass = (stats[:, i] for i in range(5))
    total = totals.astype(jnp.float32)
    row_peak = jnp.max(peak, axis=0)
    lift = jnp.exp(peak - row_peak[None])
    row_mass = jnp.sum(mass * lift, axis=0)
    floor_sum = jnp.sum(floor_mass[:, :1])
    share = (total - floor_sum) / (row_mass * total)
    scale = lift * share[None]
    block_sum = floor_mass / total[None] + mass * scale
    below = (jnp.arange(peak.shape[0]) < mine)[:, None]
    offset = jnp.sum(jnp.where(below, block_sum, 0.0), axis=0)
    target_mass = jnp.sum(floor_picked / total[None] + picked * scale, axis=0)
    my_scale = jnp.sum(jnp.where((jnp.arange(peak.shape[0]) == mine)[:, None], scale, 0.0), axis=0)
    cumulative = offset[:, None] + floor_running[:1] * (1.0 / total)[:, None] + running * my_scale[:, None]
    return cumulative, -jnp.log2(target_mass)


def local(hidden, norm_gain, head_weight, floor_counts, totals, targets):
    vocab_width = head_weight.shape[1]
    mine = lax.axis_index(BOTH)
    depth = hidden.shape[1]
    widened = hidden.astype(jnp.float32)
    square = lax.psum(jnp.sum(widened * widened, axis=1, keepdims=True), "tensor")
    mean_square = square / (depth * lax.axis_size("tensor"))
    gain = lax.dynamic_slice(norm_gain, (lax.axis_index("tensor") * depth,), (depth,))
    normed = (widened * lax.rsqrt(mean_square + epsilon) * gain.astype(jnp.float32)[None, :]).astype(jnp.bfloat16)
    normed = lax.all_gather(normed, "tensor", axis=1, tiled=True)
    normed = lax.all_gather(normed, "stream", axis=0, tiled=True)
    logits = jnp.dot(normed, head_weight, preferred_element_type=jnp.float32)
    floor = jnp.broadcast_to(floor_counts.astype(jnp.float32)[None, :], (8, vocab_width))
    target = (targets - mine * vocab_width)[:, None]
    running, floor_running, stats = post(logits, floor, target)
    stats = lax.all_gather(stats[:, :8].T, BOTH)
    return finish(stats, running, floor_running, totals, mine)


MESH = pl.DeviceIdType.MESH
PARTS = 4
SLOTS = 8
TILE = 1024


def product(left, right):
    return lax.dot_general(left, right, (((1,), (1,)), ((), ())), preferred_element_type=jnp.float32)


def head_kernel(
    devices, hidden_ref, gain_ref, weight_ref, floor_ref, target_ref, total_ref,
    running_ref, floor_running_ref, scales_ref, bits_ref,
    acts, acc, weights, lower, squares, stats, floors,
    square_send, square_recv, line_send, line_recv, first_send, first_recv,
    second_send, second_recv, pair_send, pair_recv, stats_send, stats_recv, weight_sem, out_sem,
):
    rows, depth = hidden_ref.shape
    width, tokens = acc.shape
    part = depth // PARTS
    deep = acts.shape[0] // PARTS
    line = tokens // rows // 2
    stream, tensor = lax.axis_index("stream"), lax.axis_index("tensor")
    place, side = stream // 2, stream % 2
    level, core = tensor // 2, tensor % 2
    me = stream * deep + tensor
    first_side, first_level = (side + core) % 2, (level + 1 - core) % 2
    second_side, second_level = (side + 1 - core) % 2, (level + core) % 2
    far_level = (level + 1) % 2
    first_to = (place * 2 + first_side, first_level * 2 + core)
    second_to = (place * 2 + second_side, second_level * 2 + core)
    pair_to = (stream, level * 2 + 1 - core)

    barrier = pltpu.get_barrier_semaphore()

    def greet(step, carry):
        other = (me + step) % devices
        pl.semaphore_signal(barrier, inc=1, device_id=(other // deep, other % deep), device_id_type=MESH)
        return carry

    lax.fori_loop(1, devices, greet, 0)

    def chunk_of(step):
        turn, kind = step // 4, step % 4
        at_level = (level + kind % 2) % 2
        at_core = (core + kind // 2) % 2
        return (at_level * 2 + at_core) * PARTS + turn

    def weight_copy(step):
        start = pl.multiple_of(chunk_of(step) * part, part)
        slot = step % SLOTS
        return pltpu.make_async_copy(weight_ref.at[:, pl.ds(start, part)], weights.at[slot], weight_sem.at[slot])

    steps = deep * PARTS

    def first_weights(step, carry):
        weight_copy(step).start()
        return carry

    lax.fori_loop(0, SLOTS, first_weights, 0)

    def block(at_place, at_side, at_tensor, turn):
        start = pl.multiple_of((at_place * 2 + at_side) * rows, rows)
        return acts.at[at_tensor * PARTS + turn, pl.ds(start, rows), :]

    def send(ref, send_sem, recv_sem, to):
        return pltpu.make_async_remote_copy(
            src_ref=ref, dst_ref=ref, send_sem=send_sem, recv_sem=recv_sem, device_id=to, device_id_type=MESH
        )

    def line_copy(at_place, turn, to_place):
        return send(
            block(at_place, side, tensor, turn),
            line_send.at[turn, to_place], line_recv.at[turn, at_place], (to_place * 2 + side, tensor),
        )

    def first_copy(at_place, at_side, at_level, turn):
        return send(
            block(at_place, at_side, at_level * 2 + core, turn),
            first_send.at[turn, at_place], first_recv.at[turn, at_place], first_to,
        )

    def second_copy(at_place, at_side, at_level, turn, index):
        return send(
            block(at_place, at_side, at_level * 2 + core, turn),
            second_send.at[turn, index], second_recv.at[turn, index], second_to,
        )

    def pair_copy(at_tensor, turn, index):
        return send(
            acts.at[at_tensor * PARTS + turn], pair_send.at[turn, index], pair_recv.at[turn, index], pair_to
        )

    hidden = hidden_ref[...].astype(jnp.float32)
    squares[tensor] = jnp.broadcast_to(jnp.sum(hidden * hidden, axis=1, keepdims=True), squares.shape[1:])
    pl.semaphore_wait(barrier, devices - 1)

    def square_copy(of, to):
        return send(squares.at[of], square_send.at[to], square_recv.at[of], (stream, to))

    for step in range(1, deep):
        square_copy(tensor, (tensor + step) % deep).start()

    for step in range(1, deep):
        square_copy((tensor + step) % deep, tensor).wait_recv()
    square = jnp.sum(squares[...], axis=0)[:, :1]
    factor = lax.rsqrt(square / (depth * deep) + epsilon)
    for turn in range(PARTS):
        at = slice(turn * part, (turn + 1) * part)
        gain = gain_ref[:, pl.ds(pl.multiple_of(tensor * depth + turn * part, part), part)]
        normed = hidden_ref[:, at].astype(jnp.float32) * factor * gain
        start = pl.multiple_of(stream * rows, rows)
        acts[tensor * PARTS + turn, pl.ds(start, rows), :] = normed.astype(jnp.bfloat16)
        for step in range(1, line):
            line_copy(place, turn, (place + step) % line).start()
        first_copy(place, side, level, turn).start()
        second_copy(place, side, level, turn, place).start()

    def pass_line(turn):
        def go(step, carry):
            at = (place + step) % line
            line_copy(at, turn, place).wait_recv()
            first_copy(at, side, level, turn).start()
            second_copy(at, side, level, turn, at).start()
            return carry

        lax.fori_loop(1, line, go, 0)

    def pass_first(turn):
        def go(step, carry):
            at = (place + step) % line
            first_copy(at, first_side, first_level, turn).wait_recv()
            second_copy(at, first_side, first_level, turn, line + at).start()
            return carry

        lax.fori_loop(0, line, go, 0)

    def pass_second(turn):
        def go(step, carry):
            at = (place + step) % line
            second_copy(at, second_side, second_level, turn, at).wait_recv()
            return carry

        def go_far(step, carry):
            at = (place + step) % line
            second_copy(at, (side + 1) % 2, far_level, turn, line + at).wait_recv()
            return carry

        lax.fori_loop(0, line, go, 0)
        lax.fori_loop(0, line, go_far, 0)
        pair_copy(tensor, turn, 0).start()
        pair_copy(far_level * 2 + core, turn, 1).start()

    pass_line(0)
    half = acc.shape[0] // 2 // 8 * 8
    row = lax.broadcasted_iota(jnp.int32, (BLOCK, BLOCK), 0)
    col = lax.broadcasted_iota(jnp.int32, (BLOCK, BLOCK), 1)
    lower[...] = jnp.where(col < row, 1.0, 0.0).astype(jnp.bfloat16)
    acc[:half] = jnp.zeros_like(acc[:half])
    pass_first(0)
    acc[half:] = jnp.zeros_like(acc[half:])
    pass_line(1)
    floor_total = jnp.zeros((1, 1), jnp.float32)
    for start, size in blocks_of(width):
        at = slice(start, start + size)
        piece = floor_ref[:, at].astype(jnp.float32)
        row = lax.broadcasted_iota(jnp.int32, (size, size), 0)
        col = lax.broadcasted_iota(jnp.int32, (size, size), 1)
        own = jnp.sum(jnp.where(row == col, piece, 0.0), axis=1, keepdims=True)
        below = jnp.sum(jnp.where(col < row, piece, 0.0), axis=1, keepdims=True)
        floors[at, :] = jnp.broadcast_to(own, (size, 128))
        floor_running_ref[at, :] = jnp.broadcast_to(floor_total + below, (size, 128))
        floor_total += jnp.sum(piece, axis=1, keepdims=True)
    pass_second(0)

    def multiply(pair, carry):
        turn, kind = pair // 2, pair % 2
        step = 2 * pair

        @pl.when((kind == 0) & (turn + 2 < PARTS))
        def _():
            pass_line(turn + 2)

        @pl.when((kind == 0) & (turn + 1 < PARTS))
        def _():
            pass_first(turn + 1)

        @pl.when(kind == 1)
        def _():
            pair_copy(level * 2 + 1 - core, turn, 0).wait_recv()
            pair_copy(far_level * 2 + 1 - core, turn, 1).wait_recv()

        weight_copy(step).wait()
        weight_copy(step + 1).wait()
        near, far = chunk_of(step), chunk_of(step + 1)
        slot = step % SLOTS
        for start in range(0, width, TILE):
            at = slice(start, min(start + TILE, width))
            acc[at, :] += product(weights[slot, at, :], acts[near]) + product(weights[slot + 1, at, :], acts[far])

        @pl.when(step + SLOTS < steps)
        def _():
            weight_copy(step + SLOTS).start()
            weight_copy(step + SLOTS + 1).start()

        @pl.when((kind == 1) & (turn + 1 < PARTS))
        def _():
            pass_second(turn + 1)

        return carry

    lax.fori_loop(0, steps // 2, multiply, 0)

    whole, rest = width // BLOCK, width % BLOCK

    def over_blocks(go, carry):
        def body(step, carry):
            return go(pl.multiple_of(step * BLOCK, BLOCK), BLOCK, step, carry)

        carry = lax.fori_loop(0, whole, body, carry)
        return go(whole * BLOCK, rest, whole, carry) if rest else carry

    def highest(start, size, step, carry):
        return jnp.maximum(carry, jnp.max(acc[pl.ds(start, size), :], axis=0, keepdims=True))

    peak = over_blocks(highest, jnp.full((1, tokens), -jnp.inf, jnp.float32))
    aim = target_ref[...] - me * width

    def measure(start, size, step, carry):
        mass, picked, floor_picked = carry
        at = pl.ds(start, size)
        exponent = jnp.exp(acc[at, :] - peak)
        acc[at, :] = exponent
        hit = lax.broadcasted_iota(jnp.int32, (size, tokens), 0) + start == aim
        mass += jnp.sum(exponent, axis=0, keepdims=True)
        picked += jnp.sum(jnp.where(hit, exponent, 0.0), axis=0, keepdims=True)
        floor_picked += jnp.sum(jnp.where(hit, floors[at, :1], 0.0), axis=0, keepdims=True)
        return mass, picked, floor_picked

    zero = jnp.zeros((1, tokens), jnp.float32)
    mass, picked, floor_picked = over_blocks(measure, (zero, zero, zero))
    lane = lax.broadcasted_iota(jnp.int32, (8, tokens), 0)
    value = jnp.where(lane == 0, peak, 0.0)
    value = jnp.where(lane == 1, mass, value)
    value = jnp.where(lane == 2, picked, value)
    value = jnp.where(lane == 3, floor_picked, value)
    stats[me] = jnp.where(lane == 4, floor_total, value)

    def stats_copy(of, to):
        return send(stats.at[of], stats_send.at[to], stats_recv.at[of], (to // deep, to % deep))

    def share(step, carry):
        stats_copy(me, (me + step) % devices).start()
        return carry

    lax.fori_loop(1, devices, share, 0)

    def out_copy(start, size, step):
        at = pl.ds(start, size)
        return pltpu.make_async_copy(acc.at[at, :], running_ref.at[at, :], out_sem.at[step])

    def accumulate(start, size, step, total):
        at = pl.ds(start, size)
        piece = acc[at, :]
        high = piece.astype(jnp.bfloat16)
        low = (piece - high.astype(jnp.float32)).astype(jnp.bfloat16)
        within = jnp.dot(lower[:size, :size], high, preferred_element_type=jnp.float32)
        within += jnp.dot(lower[:size, :size], low, preferred_element_type=jnp.float32)
        acc[at, :] = total + within
        out_copy(start, size, step).start()
        return total + jnp.sum(piece, axis=0, keepdims=True)

    over_blocks(accumulate, zero)

    def settle(step, carry):
        stats_copy((me + step) % devices, me).wait_recv()
        return carry

    lax.fori_loop(1, devices, settle, 0)
    peak, mass, picked, floor_picked, floor_all = (stats[:, i, :] for i in range(5))
    total = total_ref[...].astype(jnp.float32)
    lift = jnp.exp(peak - jnp.max(peak, axis=0, keepdims=True))
    row_mass = jnp.sum(mass * lift, axis=0, keepdims=True)
    floor_sum = jnp.sum(floor_all, axis=0, keepdims=True)
    scale = lift * ((total - floor_sum) / (row_mass * total))
    device = lax.broadcasted_iota(jnp.int32, peak.shape, 0)
    block_sum = floor_all / total + mass * scale
    offset = jnp.sum(jnp.where(device < me, block_sum, 0.0), axis=0, keepdims=True)
    my_scale = jnp.sum(jnp.where(device == me, scale, 0.0), axis=0, keepdims=True)
    target_mass = jnp.sum(floor_picked / total + picked * scale, axis=0, keepdims=True)
    bits_ref[...] = -(jnp.log(target_mass) / 0.6931471805599453)
    lane = lax.broadcasted_iota(jnp.int32, (8, tokens), 0)
    value = jnp.where(lane == 0, offset, 0.0)
    value = jnp.where(lane == 1, 1.0 / total, value)
    scales_ref[...] = jnp.where(lane == 2, my_scale, value)

    for step in range(1, deep):
        square_copy(tensor, (tensor + step) % deep).wait_send()

    def sent(turn, carry):
        def go_line(step, carry):
            line_copy(place, turn, (place + step) % line).wait_send()
            return carry

        def go(step, carry):
            first_copy(step, side, level, turn).wait_send()
            second_copy(step, side, level, turn, step).wait_send()
            second_copy(step, first_side, first_level, turn, line + step).wait_send()
            return carry

        lax.fori_loop(1, line, go_line, 0)
        lax.fori_loop(0, line, go, 0)
        pair_copy(tensor, turn, 0).wait_send()
        pair_copy(far_level * 2 + core, turn, 1).wait_send()
        return carry

    lax.fori_loop(0, PARTS, sent, 0)

    def stats_sent(step, carry):
        stats_copy(me, (me + step) % devices).wait_send()
        return carry

    lax.fori_loop(1, devices, stats_sent, 0)

    def out_done(start, size, step, carry):
        out_copy(start, size, step).wait()
        return carry

    over_blocks(out_done, 0)


def head(hidden, gain, weight, floor, target, total):
    rows, depth = hidden.shape
    streams, deep = lax.axis_size("stream"), lax.axis_size("tensor")
    devices, line = streams * deep, streams // 2
    tokens, width = streams * rows, weight.shape[0]
    part = depth // PARTS
    vmem = pl.BlockSpec(memory_space=pltpu.VMEM)
    anywhere = pl.BlockSpec(memory_space=pl.ANY)
    dma = pltpu.SemaphoreType.DMA
    return pl.pallas_call(
        functools.partial(head_kernel, devices),
        in_specs=[vmem, vmem, anywhere, vmem, vmem, vmem],
        out_specs=[anywhere, vmem, vmem, vmem],
        out_shape=[
            jax.ShapeDtypeStruct((width, tokens), jnp.float32),
            jax.ShapeDtypeStruct((width, 128), jnp.float32),
            jax.ShapeDtypeStruct((8, tokens), jnp.float32),
            jax.ShapeDtypeStruct((1, tokens), jnp.float32),
        ],
        scratch_shapes=[
            pltpu.VMEM((deep * PARTS, tokens, part), jnp.bfloat16),
            pltpu.VMEM((width, tokens), jnp.float32),
            pltpu.VMEM((SLOTS, width, part), jnp.bfloat16),
            pltpu.VMEM((BLOCK, BLOCK), jnp.bfloat16),
            pltpu.VMEM((deep, rows, 128), jnp.float32),
            pltpu.VMEM((devices, 8, tokens), jnp.float32),
            pltpu.VMEM((width, 128), jnp.float32),
            dma((deep,)), dma((deep,)),
            dma((PARTS, line)), dma((PARTS, line)),
            dma((PARTS, line)), dma((PARTS, line)),
            dma((PARTS, 2 * line)), dma((PARTS, 2 * line)),
            dma((PARTS, 2)), dma((PARTS, 2)),
            dma((devices,)), dma((devices,)),
            dma((SLOTS,)), dma((len(blocks_of(width)),)),
        ],
        compiler_params=pltpu.CompilerParams(
            collective_id=0, has_side_effects=True, vmem_limit_bytes=62 * 2**20
        ),
        cost_estimate=pl.CostEstimate(
            flops=2 * tokens * depth * deep * width,
            bytes_accessed=2 * depth * deep * width + 4 * tokens * width,
            transcendentals=tokens * width,
        ),
    )(hidden, gain, weight, floor, target, total)


def finish_kernel(running_ref, floor_running_ref, scales_ref, out_ref):
    offset, share, scale = (scales_ref[i : i + 1, :] for i in range(3))
    out_ref[...] = offset + floor_running_ref[:, :1] * share + running_ref[...] * scale


def finish_local(running, floor_running, scales):
    width, tokens = running.shape
    rows = 512
    tile = pl.BlockSpec((rows, tokens), lambda i: (i, 0))
    return pl.pallas_call(
        finish_kernel,
        grid=(pl.cdiv(width, rows),),
        in_specs=[tile, pl.BlockSpec((rows, 128), lambda i: (i, 0)), pl.BlockSpec((8, tokens), lambda i: (0, 0))],
        out_specs=tile,
        out_shape=jax.ShapeDtypeStruct((width, tokens), jnp.float32),
        compiler_params=pltpu.CompilerParams(vmem_limit_bytes=56 * 2**20),
        cost_estimate=pl.CostEstimate(flops=4 * tokens * width, bytes_accessed=8 * tokens * width, transcendentals=0),
    )(running, floor_running, scales)


def local_fused(hidden, norm_gain, head_weight, floor_counts, totals, targets):
    gain = norm_gain.astype(jnp.float32)[None, :]
    running, floor_running, scales, bits = head(
        hidden, gain, head_weight.T, floor_counts[None, :], targets[None, :], totals[None, :]
    )
    return finish_local(running, floor_running, scales).T, bits[0]


def solution(mesh):
    in_specs = (P("stream", "tensor"), P(), P(None, BOTH), P(BOTH), P(), P())
    out_specs = (P(None, BOTH), P())
    fused = mesh.shape["tensor"] == 4 and mesh.shape["stream"] % 2 == 0 and mesh.shape["stream"] <= 8
    body = local_fused if fused else local
    return jax.shard_map(body, mesh=mesh, in_specs=in_specs, out_specs=out_specs, check_vma=False)
```

```python
import functools

import jax
import jax.numpy as jnp
from jax import lax
from jax.experimental import pallas as pl
from jax.experimental.pallas import tpu as pltpu
from jax.sharding import PartitionSpec as P

epsilon = 1e-05
BLOCK = 256
BOTH = ("stream", "tensor")


def blocks_of(width):
    return [(start, min(BLOCK, width - start)) for start in range(0, width, BLOCK)]


def strict_upper(size):
    row = lax.broadcasted_iota(jnp.int32, (size, size), 0)
    col = lax.broadcasted_iota(jnp.int32, (size, size), 1)
    return jnp.where(row < col, 1.0, 0.0).astype(jnp.bfloat16)


def running_sum(value, upper, emit):
    rows, width = value.shape
    total = jnp.zeros((rows, 1), jnp.float32)
    for start, size in blocks_of(width):
        piece = value[:, start : start + size]
        high = piece.astype(jnp.bfloat16)
        low = (piece - high.astype(jnp.float32)).astype(jnp.bfloat16)
        within = jnp.dot(
            jnp.concatenate([high, low], axis=0), upper[:size, :size], preferred_element_type=jnp.float32
        )
        emit(start, size, total + (within[:rows] + within[rows:]))
        total += jnp.sum(piece, axis=1, keepdims=True)
    return total


def post_kernel(logits_ref, floor_ref, target_ref, running_ref, floor_running_ref, stats_ref):
    logits = logits_ref[...]
    rows, width = logits.shape
    peak = jnp.max(logits, axis=1, keepdims=True)
    exponent = jnp.exp(logits - peak)
    hit = lax.broadcasted_iota(jnp.int32, (rows, width), 1) == target_ref[...]
    picked = jnp.sum(jnp.where(hit, exponent, 0.0), axis=1, keepdims=True)
    floor = floor_ref[...]
    floor_picked = jnp.sum(jnp.where(hit, floor[:1], 0.0), axis=1, keepdims=True)

    def emit(start, size, piece):
        running_ref[:, start : start + size] = piece

    mass = running_sum(exponent, strict_upper(BLOCK), emit)

    def emit_floor(start, size, piece):
        floor_running_ref[:, start : start + size] = piece

    floor_mass = running_sum(floor, strict_upper(BLOCK), emit_floor)
    lane = lax.broadcasted_iota(jnp.int32, stats_ref.shape, 1)
    stats = jnp.where(lane == 0, peak, 0.0)
    stats = jnp.where(lane == 1, mass, stats)
    stats = jnp.where(lane == 2, picked, stats)
    stats = jnp.where(lane == 3, floor_picked, stats)
    stats = jnp.where(lane == 4, floor_mass[:1], stats)
    stats_ref[...] = stats


def post(logits, floor, target):
    tokens, width = logits.shape
    rows = 64
    return pl.pallas_call(
        post_kernel,
        grid=(tokens // rows,),
        in_specs=[
            pl.BlockSpec((rows, width), lambda i: (i, 0)),
            pl.BlockSpec((8, width), lambda i: (0, 0)),
            pl.BlockSpec((rows, 1), lambda i: (i, 0)),
        ],
        out_specs=[
            pl.BlockSpec((rows, width), lambda i: (i, 0)),
            pl.BlockSpec((8, width), lambda i: (0, 0)),
            pl.BlockSpec((rows, 128), lambda i: (i, 0)),
        ],
        out_shape=[
            jax.ShapeDtypeStruct((tokens, width), jnp.float32),
            jax.ShapeDtypeStruct((8, width), jnp.float32),
            jax.ShapeDtypeStruct((tokens, 128), jnp.float32),
        ],
        compiler_params=pltpu.CompilerParams(vmem_limit_bytes=40 * 2**20),
        cost_estimate=pl.CostEstimate(
            flops=4 * tokens * width * BLOCK, bytes_accessed=8 * tokens * width, transcendentals=tokens * width
        ),
    )(logits, floor, target)


def finish(stats, running, floor_running, totals, mine):
    peak, mass, picked, floor_picked, floor_mass = (stats[:, i] for i in range(5))
    total = totals.astype(jnp.float32)
    row_peak = jnp.max(peak, axis=0)
    lift = jnp.exp(peak - row_peak[None])
    row_mass = jnp.sum(mass * lift, axis=0)
    floor_sum = jnp.sum(floor_mass[:, :1])
    share = (total - floor_sum) / (row_mass * total)
    scale = lift * share[None]
    block_sum = floor_mass / total[None] + mass * scale
    below = (jnp.arange(peak.shape[0]) < mine)[:, None]
    offset = jnp.sum(jnp.where(below, block_sum, 0.0), axis=0)
    target_mass = jnp.sum(floor_picked / total[None] + picked * scale, axis=0)
    my_scale = jnp.sum(jnp.where((jnp.arange(peak.shape[0]) == mine)[:, None], scale, 0.0), axis=0)
    cumulative = offset[:, None] + floor_running[:1] * (1.0 / total)[:, None] + running * my_scale[:, None]
    return cumulative, -jnp.log2(target_mass)


def local(hidden, norm_gain, head_weight, floor_counts, totals, targets):
    vocab_width = head_weight.shape[1]
    mine = lax.axis_index(BOTH)
    depth = hidden.shape[1]
    widened = hidden.astype(jnp.float32)
    square = lax.psum(jnp.sum(widened * widened, axis=1, keepdims=True), "tensor")
    mean_square = square / (depth * lax.axis_size("tensor"))
    gain = lax.dynamic_slice(norm_gain, (lax.axis_index("tensor") * depth,), (depth,))
    normed = (widened * lax.rsqrt(mean_square + epsilon) * gain.astype(jnp.float32)[None, :]).astype(jnp.bfloat16)
    normed = lax.all_gather(normed, "tensor", axis=1, tiled=True)
    normed = lax.all_gather(normed, "stream", axis=0, tiled=True)
    logits = jnp.dot(normed, head_weight, preferred_element_type=jnp.float32)
    floor = jnp.broadcast_to(floor_counts.astype(jnp.float32)[None, :], (8, vocab_width))
    target = (targets - mine * vocab_width)[:, None]
    running, floor_running, stats = post(logits, floor, target)
    stats = lax.all_gather(stats[:, :8].T, BOTH)
    return finish(stats, running, floor_running, totals, mine)


MESH = pl.DeviceIdType.MESH
PARTS = 8
SLOTS = 8
TILE = 1024


def product(left, right):
    return lax.dot_general(left, right, (((1,), (1,)), ((), ())), preferred_element_type=jnp.float32)


def head_kernel(
    devices, hidden_ref, gain_ref, weight_ref, floor_ref, target_ref, total_ref,
    acc, floor_running_ref, scales_ref, bits_ref,
    acts, weights, lower, squares, stats, floors,
    square_send, square_recv, line_send, line_recv, first_send, first_recv,
    second_send, second_recv, pair_send, pair_recv, stats_send, stats_recv, weight_sem,
):
    rows, depth = hidden_ref.shape
    width, tokens = acc.shape
    part = depth // PARTS
    deep = acts.shape[0] // PARTS
    line = tokens // rows // 2
    stream, tensor = lax.axis_index("stream"), lax.axis_index("tensor")
    place, side = stream // 2, stream % 2
    level, core = tensor // 2, tensor % 2
    me = stream * deep + tensor
    first_side, first_level = (side + core) % 2, (level + 1 - core) % 2
    second_side, second_level = (side + 1 - core) % 2, (level + core) % 2
    far_level = (level + 1) % 2
    first_to = (place * 2 + first_side, first_level * 2 + core)
    second_to = (place * 2 + second_side, second_level * 2 + core)
    pair_to = (stream, level * 2 + 1 - core)

    barrier = pltpu.get_barrier_semaphore()

    def greet(step, carry):
        other = (me + step) % devices
        pl.semaphore_signal(barrier, inc=1, device_id=(other // deep, other % deep), device_id_type=MESH)
        return carry

    lax.fori_loop(1, devices, greet, 0)

    def chunk_of(step):
        turn, kind = step // 4, step % 4
        at_level = (level + kind % 2) % 2
        at_core = (core + kind // 2) % 2
        return (at_level * 2 + at_core) * PARTS + turn

    def weight_copy(step):
        start = pl.multiple_of(chunk_of(step) * part, part)
        slot = step % SLOTS
        return pltpu.make_async_copy(weight_ref.at[:, pl.ds(start, part)], weights.at[slot], weight_sem.at[slot])

    steps = deep * PARTS

    def first_weights(step, carry):
        weight_copy(step).start()
        return carry

    lax.fori_loop(0, SLOTS, first_weights, 0)

    def block(at_side, at_level, turn):
        return acts.at[(at_level * 2 + core) * PARTS + turn, at_side]

    def send(ref, send_sem, recv_sem, to):
        return pltpu.make_async_remote_copy(
            src_ref=ref, dst_ref=ref, send_sem=send_sem, recv_sem=recv_sem, device_id=to, device_id_type=MESH
        )

    def line_copy(at_place, turn, to_place):
        start = pl.multiple_of(at_place * rows, rows)
        return send(
            block(side, level, turn).at[pl.ds(start, rows), :],
            line_send.at[turn, to_place], line_recv.at[turn, at_place], (to_place * 2 + side, tensor),
        )

    def first_copy(at_side, at_level, turn):
        return send(block(at_side, at_level, turn), first_send.at[turn], first_recv.at[turn], first_to)

    def second_copy(at_side, at_level, turn, index):
        return send(
            block(at_side, at_level, turn), second_send.at[turn, index], second_recv.at[turn, index], second_to
        )

    def pair_copy(at_tensor, turn, index):
        return send(
            acts.at[at_tensor * PARTS + turn], pair_send.at[turn, index], pair_recv.at[turn, index], pair_to
        )

    hidden = hidden_ref[...].astype(jnp.float32)
    squares[tensor] = jnp.broadcast_to(jnp.sum(hidden * hidden, axis=1, keepdims=True), squares.shape[1:])
    pl.semaphore_wait(barrier, devices - 1)

    def square_copy(of, to):
        return send(squares.at[of], square_send.at[to], square_recv.at[of], (stream, to))

    for step in range(1, deep):
        square_copy(tensor, (tensor + step) % deep).start()

    for step in range(1, deep):
        square_copy((tensor + step) % deep, tensor).wait_recv()
    square = jnp.sum(squares[...], axis=0)[:, :1]
    factor = lax.rsqrt(square / (depth * deep) + epsilon)
    for turn in range(PARTS):
        at = slice(turn * part, (turn + 1) * part)
        gain = gain_ref[:, pl.ds(pl.multiple_of(tensor * depth + turn * part, part), part)]
        normed = hidden_ref[:, at].astype(jnp.float32) * factor * gain
        start = pl.multiple_of(place * rows, rows)
        acts[tensor * PARTS + turn, side, pl.ds(start, rows), :] = normed.astype(jnp.bfloat16)
        for step in range(1, line):
            line_copy(place, turn, (place + step) % line).start()

    def pass_line(turn):
        for step in range(1, line):
            line_copy((place + step) % line, turn, place).wait_recv()
        first_copy(side, level, turn).start()
        second_copy(side, level, turn, 0).start()

    def pass_first(turn):
        first_copy(first_side, first_level, turn).wait_recv()
        second_copy(first_side, first_level, turn, 1).start()

    def pass_second(turn):
        second_copy(second_side, second_level, turn, 0).wait_recv()
        second_copy((side + 1) % 2, far_level, turn, 1).wait_recv()
        pair_copy(tensor, turn, 0).start()
        pair_copy(far_level * 2 + core, turn, 1).start()

    pass_line(0)
    pass_line(1)
    half = acc.shape[0] // 2 // 8 * 8
    row = lax.broadcasted_iota(jnp.int32, (BLOCK, BLOCK), 0)
    col = lax.broadcasted_iota(jnp.int32, (BLOCK, BLOCK), 1)
    lower[...] = jnp.where(col < row, 1.0, 0.0).astype(jnp.bfloat16)
    acc[:half] = jnp.zeros_like(acc[:half])
    pass_first(0)
    acc[half:] = jnp.zeros_like(acc[half:])
    pass_line(2)
    pass_first(1)
    floor_total = jnp.zeros((1, 1), jnp.float32)
    for start, size in blocks_of(width):
        at = slice(start, start + size)
        piece = floor_ref[:, at].astype(jnp.float32)
        row = lax.broadcasted_iota(jnp.int32, (size, size), 0)
        col = lax.broadcasted_iota(jnp.int32, (size, size), 1)
        own = jnp.sum(jnp.where(row == col, piece, 0.0), axis=1, keepdims=True)
        below = jnp.sum(jnp.where(col < row, piece, 0.0), axis=1, keepdims=True)
        floors[at, :] = jnp.broadcast_to(own, (size, 128))
        floor_running_ref[at, :] = jnp.broadcast_to(floor_total + below, (size, 128))
        floor_total += jnp.sum(piece, axis=1, keepdims=True)
    pass_second(0)

    def states(chunk):
        pieces = [acts[chunk, i % 2, i // 2 * rows : (i // 2 + 1) * rows, :] for i in range(2 * line)]
        return jnp.concatenate(pieces, axis=0)

    def multiply(pair, carry):
        turn, kind = pair // 2, pair % 2
        step = 2 * pair

        @pl.when((kind == 0) & (turn + 2 < PARTS))
        def _():
            pass_first(turn + 2)

        @pl.when((kind == 0) & (turn + 3 < PARTS))
        def _():
            pass_line(turn + 3)

        @pl.when(kind == 1)
        def _():
            pair_copy(level * 2 + 1 - core, turn, 0).wait_recv()
            pair_copy(far_level * 2 + 1 - core, turn, 1).wait_recv()

        weight_copy(step).wait()
        weight_copy(step + 1).wait()
        near, far = chunk_of(step), chunk_of(step + 1)
        slot = step % SLOTS
        for start in range(0, width, TILE):
            at = slice(start, min(start + TILE, width))
            acc[at, :] += product(weights[slot, at, :], states(near)) + product(weights[slot + 1, at, :], states(far))

        @pl.when(step + SLOTS < steps)
        def _():
            weight_copy(step + SLOTS).start()
            weight_copy(step + SLOTS + 1).start()

        @pl.when((kind == 1) & (turn + 1 < PARTS))
        def _():
            pass_second(turn + 1)

        return carry

    lax.fori_loop(0, steps // 2, multiply, 0)

    whole, rest = width // BLOCK, width % BLOCK

    def over_blocks(go, carry):
        def body(step, carry):
            return go(pl.multiple_of(step * BLOCK, BLOCK), BLOCK, step, carry)

        carry = lax.fori_loop(0, whole, body, carry)
        return go(whole * BLOCK, rest, whole, carry) if rest else carry

    def highest(start, size, step, carry):
        return jnp.maximum(carry, jnp.max(acc[pl.ds(start, size), :], axis=0, keepdims=True))

    peak = over_blocks(highest, jnp.full((1, tokens), -jnp.inf, jnp.float32))
    aim = target_ref[...] - me * width

    def measure(start, size, step, carry):
        mass, picked, floor_picked = carry
        at = pl.ds(start, size)
        exponent = jnp.exp(acc[at, :] - peak)
        acc[at, :] = exponent
        hit = lax.broadcasted_iota(jnp.int32, (size, tokens), 0) + start == aim
        mass += jnp.sum(exponent, axis=0, keepdims=True)
        picked += jnp.sum(jnp.where(hit, exponent, 0.0), axis=0, keepdims=True)
        floor_picked += jnp.sum(jnp.where(hit, floors[at, :1], 0.0), axis=0, keepdims=True)
        return mass, picked, floor_picked

    zero = jnp.zeros((1, tokens), jnp.float32)
    mass, picked, floor_picked = over_blocks(measure, (zero, zero, zero))
    lane = lax.broadcasted_iota(jnp.int32, (8, tokens), 0)
    value = jnp.where(lane == 0, peak, 0.0)
    value = jnp.where(lane == 1, mass, value)
    value = jnp.where(lane == 2, picked, value)
    value = jnp.where(lane == 3, floor_picked, value)
    stats[me] = jnp.where(lane == 4, floor_total, value)

    def stats_copy(of, to):
        return send(stats.at[of], stats_send.at[to], stats_recv.at[of], (to // deep, to % deep))

    def share(step, carry):
        stats_copy(me, (me + step) % devices).start()
        return carry

    lax.fori_loop(1, devices, share, 0)

    def accumulate(start, size, step, total):
        at = pl.ds(start, size)
        piece = acc[at, :]
        high = piece.astype(jnp.bfloat16)
        low = (piece - high.astype(jnp.float32)).astype(jnp.bfloat16)
        within = jnp.dot(lower[:size, :size], high, preferred_element_type=jnp.float32)
        within += jnp.dot(lower[:size, :size], low, preferred_element_type=jnp.float32)
        acc[at, :] = total + within
        return total + jnp.sum(piece, axis=0, keepdims=True)

    over_blocks(accumulate, zero)

    def settle(step, carry):
        stats_copy((me + step) % devices, me).wait_recv()
        return carry

    lax.fori_loop(1, devices, settle, 0)
    peak, mass, picked, floor_picked, floor_all = (stats[:, i, :] for i in range(5))
    total = total_ref[...].astype(jnp.float32)
    lift = jnp.exp(peak - jnp.max(peak, axis=0, keepdims=True))
    row_mass = jnp.sum(mass * lift, axis=0, keepdims=True)
    floor_sum = jnp.sum(floor_all, axis=0, keepdims=True)
    scale = lift * ((total - floor_sum) / (row_mass * total))
    device = lax.broadcasted_iota(jnp.int32, peak.shape, 0)
    block_sum = floor_all / total + mass * scale
    offset = jnp.sum(jnp.where(device < me, block_sum, 0.0), axis=0, keepdims=True)
    my_scale = jnp.sum(jnp.where(device == me, scale, 0.0), axis=0, keepdims=True)
    target_mass = jnp.sum(floor_picked / total + picked * scale, axis=0, keepdims=True)
    bits_ref[...] = -(jnp.log(target_mass) / 0.6931471805599453)
    lane = lax.broadcasted_iota(jnp.int32, (8, tokens), 0)
    value = jnp.where(lane == 0, offset, 0.0)
    value = jnp.where(lane == 1, 1.0 / total, value)
    scales_ref[...] = jnp.where(lane == 2, my_scale, value)

    for step in range(1, deep):
        square_copy(tensor, (tensor + step) % deep).wait_send()

    def sent(turn, carry):
        for step in range(1, line):
            line_copy(place, turn, (place + step) % line).wait_send()
        first_copy(side, level, turn).wait_send()
        second_copy(side, level, turn, 0).wait_send()
        second_copy(first_side, first_level, turn, 1).wait_send()
        pair_copy(tensor, turn, 0).wait_send()
        pair_copy(far_level * 2 + core, turn, 1).wait_send()
        return carry

    lax.fori_loop(0, PARTS, sent, 0)

    def stats_sent(step, carry):
        stats_copy(me, (me + step) % devices).wait_send()
        return carry

    lax.fori_loop(1, devices, stats_sent, 0)


def head(hidden, gain, weight, floor, target, total):
    rows, depth = hidden.shape
    streams, deep = lax.axis_size("stream"), lax.axis_size("tensor")
    devices, line = streams * deep, streams // 2
    tokens, width = streams * rows, weight.shape[0]
    part = depth // PARTS
    vmem = pl.BlockSpec(memory_space=pltpu.VMEM)
    anywhere = pl.BlockSpec(memory_space=pl.ANY)
    dma = pltpu.SemaphoreType.DMA
    return pl.pallas_call(
        functools.partial(head_kernel, devices),
        in_specs=[vmem, vmem, anywhere, vmem, vmem, vmem],
        out_specs=[vmem, vmem, vmem, vmem],
        out_shape=[
            jax.ShapeDtypeStruct((width, tokens), jnp.float32),
            jax.ShapeDtypeStruct((width, 128), jnp.float32),
            jax.ShapeDtypeStruct((8, tokens), jnp.float32),
            jax.ShapeDtypeStruct((1, tokens), jnp.float32),
        ],
        scratch_shapes=[
            pltpu.VMEM((deep * PARTS, 2, line * rows, part), jnp.bfloat16),
            pltpu.VMEM((SLOTS, width, part), jnp.bfloat16),
            pltpu.VMEM((BLOCK, BLOCK), jnp.bfloat16),
            pltpu.VMEM((deep, rows, 128), jnp.float32),
            pltpu.VMEM((devices, 8, tokens), jnp.float32),
            pltpu.VMEM((width, 128), jnp.float32),
            dma((deep,)), dma((deep,)),
            dma((PARTS, line)), dma((PARTS, line)),
            dma((PARTS,)), dma((PARTS,)),
            dma((PARTS, 2)), dma((PARTS, 2)),
            dma((PARTS, 2)), dma((PARTS, 2)),
            dma((devices,)), dma((devices,)),
            dma((SLOTS,)),
        ],
        compiler_params=pltpu.CompilerParams(
            collective_id=0, has_side_effects=True, vmem_limit_bytes=42 * 2**20
        ),
        cost_estimate=pl.CostEstimate(
            flops=2 * tokens * depth * deep * width,
            bytes_accessed=2 * depth * deep * width + 4 * tokens * width,
            transcendentals=tokens * width,
        ),
    )(hidden, gain, weight, floor, target, total)


def finish_kernel(running_ref, floor_running_ref, scales_ref, out_ref):
    offset, share, scale = (scales_ref[i : i + 1, :] for i in range(3))
    out_ref[...] = offset + floor_running_ref[:, :1] * share + running_ref[...] * scale


def finish_local(running, floor_running, scales):
    width, tokens = running.shape
    rows = 512
    tile = pl.BlockSpec((rows, tokens), lambda i: (i, 0))
    return pl.pallas_call(
        finish_kernel,
        grid=(pl.cdiv(width, rows),),
        in_specs=[tile, pl.BlockSpec((rows, 128), lambda i: (i, 0)), pl.BlockSpec((8, tokens), lambda i: (0, 0))],
        out_specs=tile,
        out_shape=jax.ShapeDtypeStruct((width, tokens), jnp.float32),
        compiler_params=pltpu.CompilerParams(vmem_limit_bytes=12 * 2**20),
        cost_estimate=pl.CostEstimate(flops=4 * tokens * width, bytes_accessed=8 * tokens * width, transcendentals=0),
    )(running, floor_running, scales)


def local_fused(hidden, norm_gain, head_weight, floor_counts, totals, targets):
    gain = norm_gain.astype(jnp.float32)[None, :]
    running, floor_running, scales, bits = head(
        hidden, gain, head_weight.T, floor_counts[None, :], targets[None, :], totals[None, :]
    )
    return finish_local(running, floor_running, scales).T, bits[0]


def solution(mesh):
    in_specs = (P("stream", "tensor"), P(), P(None, BOTH), P(BOTH), P(), P())
    out_specs = (P(None, BOTH), P())
    fused = mesh.shape["tensor"] == 4 and mesh.shape["stream"] % 2 == 0 and mesh.shape["stream"] <= 8
    body = local_fused if fused else local
    return jax.shard_map(body, mesh=mesh, in_specs=in_specs, out_specs=out_specs, check_vma=False)
```
